32 devices in a mesh: pipe: 4 (over y, core), ctx: 8 (over z, x).
Axes of the slice: x: 2, y: 2, z: 4, core: 2. Of those that a mesh axis runs over, the one named last changes fastest.
Arguments:
- incoming: bfloat16 [4, 1024, 1024], P('pipe', 'ctx'), may hold values from -6 to 6
- fresh: bfloat16 [1024, 1024], P('ctx'), may hold values from -6 to 6
- w_uvqk: bfloat16 [4, 1024, 2048], P('pipe'), may hold values from -0.1875 to 0.1875
- w_out: bfloat16 [4, 512, 1024], P('pipe'), may hold values from -0.25 to 0.25
- cache_kv: bfloat16 [4, 2, 128, 1024], P('pipe', None, 'ctx'), may hold values from -6 to 6
- rows_user: int32 [5, 1024], P(None, 'ctx'), may hold values from 0 to 3, never falling along the last dimension, each value on 1 to 512 neighbouring positions
- cache_len: int32 [5, 4], replicated, may hold values from 1 to 64, 128 in all within a row
Outputs:
- section_out: bfloat16 [4, 2, 1024, 1024], P('pipe', None, 'ctx')
The draws below stay inside these ranges and needn't reach their ends.
Inputs may be any that keep to these rules, and one draw needn't show every extreme that they name: `rows_user`: each micro-batch's row users never fall along the events; every user has at least one event. `cache_len`: each micro-batch's row sums to 128.
All inputs are finite; a program needn't handle non-finite values.
Results may differ from the reference program's by a relative error of at most 0.0085.
Values may be sent and summed in bfloat16 or wider, within the bound.
A program may use at most 64 MiB of HBM per device.

```python
import math
import jax
import jax.numpy as jnp
import numpy as np
from jax import lax

D = 1024
HEADS = 4
HD = 128
HW = 512
TOK_DEV = 128
USERS = 4
STEPS = 2
SECTIONS = 4
BATCHES = 5
TOKENS = 1024
CACHE = 128
N_CTX = 8


def block_levels(key, shape, cuts, smallest, top_value):
    loudness = 1.0
    for axis_at, shards_of in cuts:
        steps = jax.random.uniform(jax.random.fold_in(jax.random.fold_in(key, 6), axis_at), (shards_of,), jnp.float32, smallest / len(cuts), top_value / len(cuts))
        loudness = loudness * jnp.repeat(jnp.exp(steps), shape[axis_at] // shards_of).reshape((-1,) + (1,) * (len(shape) - 1 - axis_at))
    return loudness


def split_up(count, total, limit, skew):
    weights = [(1 << 20) // math.isqrt(standing ** skew) + 1 for standing in range(2, count + 1)]
    spare, counts = total - limit - (count - 1), [1] * (count - 1)
    while spare > 0:
        candidates = [i for i in range(count - 1) if counts[i] < limit]
        pool, budget = sum([weights[i] for i in candidates]), spare
        for i in candidates:
            addition = min(limit - counts[i], max(1, budget * weights[i] // pool), spare)
            counts[i] = counts[i] + addition
            spare = spare - addition
    return np.array([limit] + counts)


def uneven(key, count, total, limit, lean):
    if count == 2:
        one = jax.random.randint(key, (), max(1, total - limit), min(limit, total - 1) + 1)
        return jnp.stack([one, total - one])
    sizes = jnp.asarray(split_up(count, total, limit, lean), jnp.int32)
    twos = (count - 1) // 2
    donor, sink = sizes[1:1 + 2 * twos:2], sizes[2:2 + 2 * twos:2]
    slack = jnp.minimum(donor - 1, limit - sink)
    moved = jax.random.randint(jax.random.fold_in(key, 1), (twos,), 0, 1 << 20) % (slack + 1)
    sizes = sizes.at[1:1 + 2 * twos:2].set(donor - moved).at[2:2 + 2 * twos:2].set(sink + moved)
    return sizes[jax.random.permutation(jax.random.fold_in(key, 2), count)]


def bell_draw(own_key, extent, scale, reach, split=(), held_as=jnp.bfloat16):
    array = jax.random.normal(own_key, extent, jnp.float32) * scale
    if len(split) > 0:
        array = block_levels(own_key, extent, split, -0.22, 0.18) * array
    return jnp.clip(array, min=-reach, max=reach).astype(held_as)


def setup_inputs(seed: int = 0) -> dict:
    seeds = jax.random.split(jax.random.key(seed), 8)
    return {
        "incoming": bell_draw(seeds[0], (SECTIONS, TOKENS, D), 1.0, 6.0, ((0, 4), (1, 8))),
        "fresh": bell_draw(seeds[1], (TOKENS, D), 1.0, 6.0, ((0, 8),)),
        "w_uvqk": bell_draw(seeds[2], (SECTIONS, D, 4 * HW), D ** -0.5, 0.1875, ((0, 4),)),
        "w_out": bell_draw(seeds[3], (SECTIONS, HW, D), HW ** -0.5, 0.25, ((0, 4),)),
        "cache_kv": bell_draw(seeds[4], (SECTIONS, STEPS, CACHE, 2 * HW), 1.0, 6.0, ((0, 4), (2, 8))),
        "rows_user": jax.vmap(lambda own: jnp.searchsorted(jnp.cumsum(uneven(own, USERS, TOKENS, TOKENS // 2, 2)), jnp.arange(TOKENS), side="right"))(jax.random.split(seeds[5], BATCHES)).reshape((BATCHES, TOKENS)).astype(jnp.int32),
        "cache_len": jax.vmap(lambda own: uneven(own, USERS, CACHE, CACHE // 2, 1))(jax.random.split(seeds[6], BATCHES)).reshape((BATCHES, USERS)).astype(jnp.int32),
    }


def normalize(values):
    center = lax.optimization_barrier(jnp.mean(values, axis=-1, keepdims=True))
    shifted = values - center
    spread = lax.optimization_barrier(jnp.mean(shifted * shifted, axis=-1, keepdims=True))
    return shifted * lax.rsqrt(spread + 1e-06)

def owners(positions, lengths):
    bounds = jnp.cumsum(lengths.astype(jnp.int32)).astype(jnp.int32)
    return lax.optimization_barrier(jnp.sum((positions[:, None] >= bounds[None, :-1]).astype(jnp.int32), axis=1)).astype(jnp.int32)

def layer(inputs, w_in, w_back, cache_rows, users, lengths):
    width = w_back.shape[0]
    scale = HD ** (-0.5)
    normed = normalize(inputs.astype(jnp.float32)).astype(jnp.bfloat16)
    projected = jax.nn.silu(jnp.dot(normed, w_in, preferred_element_type=jnp.float32)).astype(jnp.bfloat16)
    gate_u = projected[:, :width]
    cache_user = owners(jnp.arange(CACHE, dtype=jnp.int32), lengths)
    cache_keys = cache_rows[:, :width].astype(jnp.float32).reshape(CACHE, HEADS, HD)
    cache_values = cache_rows[:, width:].astype(jnp.float32).reshape(CACHE, HEADS, HD)
    row_index = jnp.arange(TOK_DEV, dtype=jnp.int32)
    causal = row_index[None, :] <= row_index[:, None]

    def block_term(packed):
        block_q, block_k, block_v, block_users = packed
        query = block_q.astype(jnp.float32).reshape(TOK_DEV, HEADS, HD)
        own_keys = block_k.astype(jnp.float32).reshape(TOK_DEV, HEADS, HD)
        own_values = block_v.astype(jnp.float32).reshape(TOK_DEV, HEADS, HD)
        scores = jnp.einsum('thd,chd->htc', query, cache_keys)
        allowed = (block_users[:, None] == cache_user[None, :]).astype(jnp.float32)
        weights = (jax.nn.silu(scale * scores) * allowed[None]).astype(jnp.bfloat16).astype(jnp.float32)
        total = jnp.einsum('htc,chd->thd', weights, cache_values)
        local_scores = jnp.einsum('thd,rhd->htr', query, own_keys)
        local_allowed = (causal & (block_users[:, None] == block_users[None, :])).astype(jnp.float32)
        local_weights = (jax.nn.silu(scale * local_scores) * local_allowed[None]).astype(jnp.bfloat16).astype(jnp.float32)
        total = total + jnp.einsum('htr,rhd->thd', local_weights, own_values)
        return total.reshape(TOK_DEV, width)
    packed = (projected[:, width:2 * width].reshape(N_CTX, TOK_DEV, width), projected[:, 2 * width:3 * width].reshape(N_CTX, TOK_DEV, width), projected[:, 3 * width:].reshape(N_CTX, TOK_DEV, width), users.reshape(N_CTX, TOK_DEV))
    attn = lax.map(block_term, packed).reshape(TOKENS, width)
    mixed = (normalize(attn) * gate_u.astype(jnp.float32)).astype(jnp.bfloat16)
    return (jnp.dot(mixed, w_back, preferred_element_type=jnp.float32) + inputs.astype(jnp.float32)).astype(jnp.bfloat16)

def reference(incoming, fresh, w_uvqk, w_out, cache_kv, rows_user, cache_len):
    first = []
    for section in range(SECTIONS):
        batch = SECTIONS - 1 - section
        first.append(layer(incoming[section], w_uvqk[section], w_out[section], cache_kv[section, 0], rows_user[batch], cache_len[batch]))
    second = []
    for section in range(SECTIONS):
        batch = SECTIONS - section
        source = fresh if section == 0 else first[section - 1]
        second.append(layer(source, w_uvqk[section], w_out[section], cache_kv[section, 1], rows_user[batch], cache_len[batch]))
    return jnp.stack([jnp.stack([first[section], second[section]]) for section in range(SECTIONS)])
```

```python
import functools

import jax
import jax.numpy as jnp
from jax import lax
from jax.experimental import pallas as pl
from jax.experimental.pallas import tpu as pltpu
from jax.sharding import PartitionSpec as P

HEADS = 4
STEPS = 2
CHUNKS = 4
MESH = pl.DeviceIdType.MESH


def normalize(values):
    center = jnp.mean(values, axis=-1, keepdims=True)
    shifted = values - center
    spread = jnp.mean(shifted * shifted, axis=-1, keepdims=True)
    return shifted * lax.rsqrt(spread + 1e-06)


def silu(values):
    half = 0.5 * values
    return half + half * jnp.tanh(half)


def kernel(
    sections, n, stride,
    incoming, fresh, w_in, w_out, cache, users_ref, lengths_ref,
    out,
    x_buf, w_buf, wo_buf, kv, q_buf, result,
    load_sem, w_sem, out_sem, own_sem, cache_send, cache_recv, relay_send, relay_recv,
):
    section = lax.axis_index("pipe")
    me = lax.axis_index("ctx")
    rows = x_buf.shape[1]
    width = wo_buf.shape[0]
    depth = wo_buf.shape[1]
    piece = depth // CHUNKS
    part = cache.shape[2]
    cached = n * part
    head = width // HEADS
    lines = n // stride
    first = section == 0
    last = section == sections - 1

    x_load = pltpu.make_async_copy(incoming.at[0], x_buf.at[0], load_sem.at[0])
    x_load.start()
    fresh_load = pltpu.make_async_copy(fresh, x_buf.at[1], load_sem.at[1])

    @pl.when(first)
    def _():
        fresh_load.start()

    def w_load(block):
        columns = pl.ds(block * width, width)
        return pltpu.make_async_copy(
            w_in.at[0, :, columns], w_buf.at[:, columns], w_sem.at[block]
        )

    wo_load = pltpu.make_async_copy(w_out.at[0], wo_buf, load_sem.at[2])
    for block in (2, 3, 1, 0):
        w_load(block).start()
    wo_load.start()

    def place(owner):
        return pl.ds(pl.multiple_of(owner * part, part), part)

    own = [
        pltpu.make_async_copy(cache.at[0, t], kv.at[t, place(me), :], own_sem.at[t])
        for t in range(STEPS)
    ]
    for copy in own:
        copy.start()

    lane = lax.rem(me, stride)
    group = me - lane

    def along(hop):
        return lax.rem(me + hop * stride, n)

    def beside(hop):
        return group + lax.rem(lane + hop, stride)

    barrier = pltpu.get_barrier_semaphore()
    for hop in range(1, lines):
        pl.semaphore_signal(barrier, inc=1, device_id={"ctx": along(hop)}, device_id_type=MESH)
    for hop in range(1, stride):
        pl.semaphore_signal(barrier, inc=1, device_id={"ctx": beside(hop)}, device_id_type=MESH)

    @pl.when(jnp.logical_not(last))
    def _():
        pl.semaphore_signal(barrier, inc=1, device_id={"pipe": section + 1}, device_id_type=MESH)

    @pl.when(jnp.logical_not(first))
    def _():
        pl.semaphore_signal(barrier, inc=1, device_id={"pipe": section - 1}, device_id_type=MESH)

    ends = jnp.where(first, 1, 0) + jnp.where(last, 1, 0)
    pl.semaphore_wait(barrier, lines - 1 + stride - 1 + 2 - ends)

    def spread(t, hop):
        slot = hop * stride
        return pltpu.make_async_remote_copy(
            src_ref=cache.at[0, t],
            dst_ref=kv.at[t, place(me), :],
            send_sem=cache_send.at[t, slot],
            recv_sem=cache_recv.at[t, slot],
            device_id={"ctx": along(hop)},
            device_id_type=MESH,
        )

    def spread_arrival(t, hop):
        slot = hop * stride
        owner = lax.rem(me + (lines - hop) * stride, n)
        return pltpu.make_async_remote_copy(
            src_ref=cache.at[0, t],
            dst_ref=kv.at[t, place(owner), :],
            send_sem=cache_send.at[t, slot],
            recv_sem=cache_recv.at[t, slot],
            device_id={"ctx": along(hop)},
            device_id_type=MESH,
        )

    def forward(t, hop, side):
        slot = hop * stride + side
        owner = lax.rem(me + (lines - hop) * stride, n)
        source = cache.at[0, t] if hop == 0 else kv.at[t, place(owner), :]
        return pltpu.make_async_remote_copy(
            src_ref=source,
            dst_ref=kv.at[t, place(owner), :],
            send_sem=cache_send.at[t, slot],
            recv_sem=cache_recv.at[t, slot],
            device_id={"ctx": beside(side)},
            device_id_type=MESH,
        )

    def forward_arrival(t, hop, side):
        slot = hop * stride + side
        owner = lax.rem(beside(stride - side) + (lines - hop) * stride, n)
        return pltpu.make_async_remote_copy(
            src_ref=cache.at[0, t],
            dst_ref=kv.at[t, place(owner), :],
            send_sem=cache_send.at[t, slot],
            recv_sem=cache_recv.at[t, slot],
            device_id={"ctx": beside(side)},
            device_id_type=MESH,
        )

    def send_own(t):
        for hop in range(1, lines):
            spread(t, hop).start()
        for side in range(1, stride):
            forward(t, 0, side).start()

    def pass_on(t):
        for hop in range(1, lines):
            spread_arrival(t, hop).wait_recv()
            for side in range(1, stride):
                forward(t, hop, side).start()

    def arrived(t):
        own[t].wait()
        for hop in range(lines):
            for side in range(1, stride):
                forward_arrival(t, hop, side).wait_recv()

    def relay(c):
        columns = pl.ds(c * piece, piece)
        return pltpu.make_async_remote_copy(
            src_ref=result.at[0, :, columns],
            dst_ref=x_buf.at[1, :, columns],
            send_sem=relay_send.at[c],
            recv_sem=relay_recv.at[c],
            device_id={"pipe": lax.rem(section + 1, sections)},
            device_id_type=MESH,
        )

    def store(t):
        return pltpu.make_async_copy(result.at[t], out.at[0, t], out_sem.at[t])

    def project(normed, block):
        return silu(
            jnp.dot(
                normed,
                w_buf[:, block * width : (block + 1) * width],
                preferred_element_type=jnp.float32,
            )
        ).astype(jnp.bfloat16)

    def allowed_rows(t):
        batch = sections - 1 - section + t
        users = jnp.broadcast_to(users_ref[pl.ds(batch, 1), :], (rows, rows))
        mine = users.T
        row = lax.broadcasted_iota(jnp.int32, (rows, rows), 0)
        column = lax.broadcasted_iota(jnp.int32, (rows, rows), 1)
        new = jnp.where((users == mine) & (column <= row), 1.0, 0.0)
        position = lax.broadcasted_iota(jnp.int32, (rows, cached), 1)
        owner = jnp.zeros((rows, cached), jnp.int32)
        bound = jnp.int32(0)
        for user in range(lengths_ref.shape[1] - 1):
            bound = bound + lengths_ref[batch, user]
            owner = owner + jnp.where(position >= bound, 1, 0)
        old = jnp.where(owner == mine[:, :1], 1.0, 0.0)
        return jnp.concatenate([old, new], axis=1)

    send_own(0)
    for t in range(STEPS):
        allowed = allowed_rows(t)
        if t == 0:
            x_load.wait()
        else:
            @pl.when(first)
            def _():
                fresh_load.wait()

            @pl.when(jnp.logical_not(first))
            def _():
                for c in range(CHUNKS):
                    relay(c).wait_recv()

        normed = normalize(x_buf[t].astype(jnp.float32)).astype(jnp.bfloat16)
        for block, into in ((2, 0), (3, 1)):
            if t == 0:
                w_load(block).wait()
            kv[t, cached:, into * width : (into + 1) * width] = project(normed, block)
        if t == 0:
            pass_on(0)
            send_own(1)
            w_load(1).wait()
        q_buf[...] = project(normed, 1)
        if t == 0:
            w_load(0).wait()
        gate = project(normed, 0)
        arrived(t)
        heads = []
        for h in range(HEADS):
            low, high = h * head, (h + 1) * head
            scores = lax.dot_general(
                q_buf[:, low:high],
                kv[t, :, low:high],
                (((1,), (1,)), ((), ())),
                preferred_element_type=jnp.float32,
            )
            weights = (silu(head ** (-0.5) * scores) * allowed).astype(jnp.bfloat16)
            heads.append(
                jnp.dot(
                    weights,
                    kv[t, :, width + low : width + high],
                    preferred_element_type=jnp.float32,
                )
            )
        attn = jnp.concatenate(heads, axis=1)
        mixed = (normalize(attn) * gate.astype(jnp.float32)).astype(jnp.bfloat16)
        if t == 0:
            wo_load.wait()
        for c in range(CHUNKS):
            low, high = c * piece, (c + 1) * piece
            result[t, :, low:high] = (
                jnp.dot(mixed, wo_buf[:, low:high], preferred_element_type=jnp.float32)
                + x_buf[t, :, low:high].astype(jnp.float32)
            ).astype(jnp.bfloat16)
            if t == 0:
                @pl.when(jnp.logical_not(last))
                def _():
                    relay(c).start()
        store(t).start()
        if t == 0:
            pass_on(1)

    for t in range(STEPS):
        store(t).wait()
        for hop in range(lines):
            if hop > 0:
                spread(t, hop).wait_send()
            for side in range(1, stride):
                forward(t, hop, side).wait_send()

    @pl.when(jnp.logical_not(last))
    def _():
        for c in range(CHUNKS):
            relay(c).wait_send()


def body(incoming, fresh, w_uvqk, w_out, cache_kv, rows_user, cache_len):
    sections = lax.axis_size("pipe")
    n = lax.axis_size("ctx")
    stride = 2 if n % 2 == 0 else 1
    rows, depth = fresh.shape
    width = w_out.shape[1]
    part = cache_kv.shape[2]
    anywhere = pl.BlockSpec(memory_space=pl.ANY)
    dma = pltpu.SemaphoreType.DMA
    return pl.pallas_call(
        functools.partial(kernel, sections, n, stride),
        out_shape=jax.ShapeDtypeStruct((1, STEPS, rows, depth), jnp.bfloat16),
        in_specs=[anywhere] * 5
        + [
            pl.BlockSpec(memory_space=pltpu.VMEM),
            pl.BlockSpec(memory_space=pltpu.SMEM),
        ],
        out_specs=anywhere,
        scratch_shapes=[
            pltpu.VMEM((STEPS, rows, depth), jnp.bfloat16),
            pltpu.VMEM((depth, 4 * width), jnp.bfloat16),
            pltpu.VMEM((width, depth), jnp.bfloat16),
            pltpu.VMEM((STEPS, n * part + rows, 2 * width), jnp.bfloat16),
            pltpu.VMEM((rows, width), jnp.bfloat16),
            pltpu.VMEM((STEPS, rows, depth), jnp.bfloat16),
            dma((3,)),
            dma((4,)),
            dma((STEPS,)),
            dma((STEPS,)),
            dma((STEPS, n)),
            dma((STEPS, n)),
            dma((CHUNKS,)),
            dma((CHUNKS,)),
        ],
        compiler_params=pltpu.CompilerParams(
            collective_id=0, has_side_effects=True, vmem_limit_bytes=40 * 2**20
        ),
    )(incoming, fresh, w_uvqk, w_out, cache_kv, rows_user, cache_len)


def solution(mesh):
    in_specs = (
        P("pipe", "ctx", None),
        P("ctx", None),
        P("pipe", None, None),
        P("pipe", None, None),
        P("pipe", None, "ctx", None),
        P(None, "ctx"),
        P(),
    )
    out_specs = P("pipe", None, "ctx", None)
    return jax.shard_map(body, mesh=mesh, in_specs=in_specs, out_specs=out_specs, check_vma=False)
```

```python
import functools

import jax
import jax.numpy as jnp
from jax import lax
from jax.experimental import pallas as pl
from jax.experimental.pallas import tpu as pltpu
from jax.sharding import PartitionSpec as P

HEADS = 4
STEPS = 2
CHUNKS = 4
MESH = pl.DeviceIdType.MESH


def normalize(values):
    center = jnp.mean(values, axis=-1, keepdims=True)
    shifted = values - center
    spread = jnp.mean(shifted * shifted, axis=-1, keepdims=True)
    return shifted * lax.rsqrt(spread + 1e-06)


def silu(values):
    half = 0.5 * values
    return half + half * jnp.tanh(half)


def kernel(
    sections, n, stride,
    incoming, fresh, w_in, w_out, cache, users_in, lengths_in,
    result,
    x_buf, w_buf, wo_buf, kv, q_buf, users_ref, lengths_ref,
    load_sem, w_sem, own_sem, cache_send, cache_recv, relay_send, relay_recv,
):
    section = lax.axis_index("pipe")
    me = lax.axis_index("ctx")
    rows = x_buf.shape[1]
    width = wo_buf.shape[0]
    depth = wo_buf.shape[1]
    piece = depth // CHUNKS
    part = cache.shape[2]
    cached = n * part
    head = width // HEADS
    lines = n // stride
    first = section == 0
    last = section == sections - 1

    x_load = pltpu.make_async_copy(incoming.at[0], x_buf.at[0], load_sem.at[0])
    x_load.start()
    users_load = pltpu.make_async_copy(users_in, users_ref, load_sem.at[3])
    lengths_load = pltpu.make_async_copy(lengths_in, lengths_ref, load_sem.at[4])
    users_load.start()
    lengths_load.start()
    fresh_load = pltpu.make_async_copy(fresh, x_buf.at[1], load_sem.at[1])

    @pl.when(first)
    def _():
        fresh_load.start()

    def w_load(block):
        columns = pl.ds(block * width, width)
        return pltpu.make_async_copy(
            w_in.at[0, :, columns], w_buf.at[:, columns], w_sem.at[block]
        )

    wo_load = pltpu.make_async_copy(w_out.at[0], wo_buf, load_sem.at[2])
    for block in (2, 3, 1, 0):
        w_load(block).start()
    wo_load.start()

    def place(owner):
        return pl.ds(pl.multiple_of(owner * part, part), part)

    own = [
        pltpu.make_async_copy(cache.at[0, t], kv.at[t, place(me), :], own_sem.at[t])
        for t in range(STEPS)
    ]
    for copy in own:
        copy.start()

    lane = lax.rem(me, stride)
    group = me - lane

    def along(hop):
        return lax.rem(me + hop * stride, n)

    def beside(hop):
        return group + lax.rem(lane + hop, stride)

    barrier = pltpu.get_barrier_semaphore()
    for hop in range(1, lines):
        pl.semaphore_signal(barrier, inc=1, device_id={"ctx": along(hop)}, device_id_type=MESH)
    for hop in range(1, stride):
        pl.semaphore_signal(barrier, inc=1, device_id={"ctx": beside(hop)}, device_id_type=MESH)

    @pl.when(jnp.logical_not(last))
    def _():
        pl.semaphore_signal(barrier, inc=1, device_id={"pipe": section + 1}, device_id_type=MESH)

    @pl.when(jnp.logical_not(first))
    def _():
        pl.semaphore_signal(barrier, inc=1, device_id={"pipe": section - 1}, device_id_type=MESH)

    ends = jnp.where(first, 1, 0) + jnp.where(last, 1, 0)
    pl.semaphore_wait(barrier, lines - 1 + stride - 1 + 2 - ends)

    def spread(t, hop):
        slot = hop * stride
        return pltpu.make_async_remote_copy(
            src_ref=cache.at[0, t],
            dst_ref=kv.at[t, place(me), :],
            send_sem=cache_send.at[t, slot],
            recv_sem=cache_recv.at[t, slot],
            device_id={"ctx": along(hop)},
            device_id_type=MESH,
        )

    def spread_arrival(t, hop):
        slot = hop * stride
        owner = lax.rem(me + (lines - hop) * stride, n)
        return pltpu.make_async_remote_copy(
            src_ref=cache.at[0, t],
            dst_ref=kv.at[t, place(owner), :],
            send_sem=cache_send.at[t, slot],
            recv_sem=cache_recv.at[t, slot],
            device_id={"ctx": along(hop)},
            device_id_type=MESH,
        )

    def forward(t, hop, side):
        slot = hop * stride + side
        owner = lax.rem(me + (lines - hop) * stride, n)
        source = cache.at[0, t] if hop == 0 else kv.at[t, place(owner), :]
        return pltpu.make_async_remote_copy(
            src_ref=source,
            dst_ref=kv.at[t, place(owner), :],
            send_sem=cache_send.at[t, slot],
            recv_sem=cache_recv.at[t, slot],
            device_id={"ctx": beside(side)},
            device_id_type=MESH,
        )

    def forward_arrival(t, hop, side):
        slot = hop * stride + side
        owner = lax.rem(beside(stride - side) + (lines - hop) * stride, n)
        return pltpu.make_async_remote_copy(
            src_ref=cache.at[0, t],
            dst_ref=kv.at[t, place(owner), :],
            send_sem=cache_send.at[t, slot],
            recv_sem=cache_recv.at[t, slot],
            device_id={"ctx": beside(side)},
            device_id_type=MESH,
        )

    def send_own(t):
        for hop in range(1, lines):
            spread(t, hop).start()
        for side in range(1, stride):
            forward(t, 0, side).start()

    def pass_on(t):
        for hop in range(1, lines):
            spread_arrival(t, hop).wait_recv()
            for side in range(1, stride):
                forward(t, hop, side).start()

    def arrived(t):
        own[t].wait()
        for hop in range(lines):
            for side in range(1, stride):
                forward_arrival(t, hop, side).wait_recv()

    def relay(c):
        columns = pl.ds(c * piece, piece)
        return pltpu.make_async_remote_copy(
            src_ref=result.at[0, 0, :, columns],
            dst_ref=x_buf.at[1, :, columns],
            send_sem=relay_send.at[c],
            recv_sem=relay_recv.at[c],
            device_id={"pipe": lax.rem(section + 1, sections)},
            device_id_type=MESH,
        )

    def project(normed, block):
        return silu(
            jnp.dot(
                normed,
                w_buf[:, block * width : (block + 1) * width],
                preferred_element_type=jnp.float32,
            )
        ).astype(jnp.bfloat16)

    def allowed_rows(t):
        batch = sections - 1 - section + t
        users = jnp.broadcast_to(users_ref[pl.ds(batch, 1), :], (rows, rows))
        mine = users.T
        row = lax.broadcasted_iota(jnp.int32, (rows, rows), 0)
        column = lax.broadcasted_iota(jnp.int32, (rows, rows), 1)
        new = jnp.where((users == mine) & (column <= row), 1.0, 0.0)
        position = lax.broadcasted_iota(jnp.int32, (rows, cached), 1)
        owner = jnp.zeros((rows, cached), jnp.int32)
        bound = jnp.int32(0)
        for user in range(lengths_ref.shape[0] - 1):
            bound = bound + lengths_ref[user, batch]
            owner = owner + jnp.where(position >= bound, 1, 0)
        old = jnp.where(owner == mine[:, :1], 1.0, 0.0)
        return jnp.concatenate([old, new], axis=1)

    send_own(0)
    send_own(1)
    users_load.wait()
    lengths_load.wait()
    for t in range(STEPS):
        allowed = allowed_rows(t)
        if t == 0:
            x_load.wait()
        else:
            @pl.when(first)
            def _():
                fresh_load.wait()

            @pl.when(jnp.logical_not(first))
            def _():
                for c in range(CHUNKS):
                    relay(c).wait_recv()

        normed = normalize(x_buf[t].astype(jnp.float32)).astype(jnp.bfloat16)
        for block, into in ((2, 0), (3, 1)):
            if t == 0:
                w_load(block).wait()
            kv[t, cached:, into * width : (into + 1) * width] = project(normed, block)
        if t == 0:
            pass_on(0)
            w_load(1).wait()
        q_buf[...] = project(normed, 1)
        if t == 0:
            w_load(0).wait()
        gate = project(normed, 0)
        arrived(t)
        heads = []
        for h in range(HEADS):
            low, high = h * head, (h + 1) * head
            scores = lax.dot_general(
                q_buf[:, low:high],
                kv[t, :, low:high],
                (((1,), (1,)), ((), ())),
                preferred_element_type=jnp.float32,
            )
            weights = (silu(head ** (-0.5) * scores) * allowed).astype(jnp.bfloat16)
            heads.append(
                jnp.dot(
                    weights,
                    kv[t, :, width + low : width + high],
                    preferred_element_type=jnp.float32,
                )
            )
        attn = jnp.concatenate(heads, axis=1)
        mixed = (normalize(attn) * gate.astype(jnp.float32)).astype(jnp.bfloat16)
        if t == 0:
            wo_load.wait()
        for c in range(CHUNKS):
            low, high = c * piece, (c + 1) * piece
            result[0, t, :, low:high] = (
                jnp.dot(mixed, wo_buf[:, low:high], preferred_element_type=jnp.float32)
                + x_buf[t, :, low:high].astype(jnp.float32)
            ).astype(jnp.bfloat16)
            if t == 0:
                @pl.when(jnp.logical_not(last))
                def _():
                    relay(c).start()
        if t == 0:
            pass_on(1)

    for t in range(STEPS):
        for hop in range(lines):
            if hop > 0:
                spread(t, hop).wait_send()
            for side in range(1, stride):
                forward(t, hop, side).wait_send()

    @pl.when(jnp.logical_not(last))
    def _():
        for c in range(CHUNKS):
            relay(c).wait_send()


def body(incoming, fresh, w_uvqk, w_out, cache_kv, rows_user, cache_len):
    sections = lax.axis_size("pipe")
    n = lax.axis_size("ctx")
    stride = 2 if n % 2 == 0 else 1
    rows, depth = fresh.shape
    width = w_out.shape[1]
    part = cache_kv.shape[2]
    anywhere = pl.BlockSpec(memory_space=pltpu.HBM)
    dma = pltpu.SemaphoreType.DMA
    return pl.pallas_call(
        functools.partial(kernel, sections, n, stride),
        out_shape=jax.ShapeDtypeStruct((1, STEPS, rows, depth), jnp.bfloat16),
        in_specs=[anywhere] * 7,
        out_specs=pl.BlockSpec(memory_space=pltpu.VMEM),
        scratch_shapes=[
            pltpu.VMEM((STEPS, rows, depth), jnp.bfloat16),
            pltpu.VMEM((depth, 4 * width), jnp.bfloat16),
            pltpu.VMEM((width, depth), jnp.bfloat16),
            pltpu.VMEM((STEPS, n * part + rows, 2 * width), jnp.bfloat16),
            pltpu.VMEM((rows, width), jnp.bfloat16),
            pltpu.VMEM(rows_user.shape, jnp.int32),
            pltpu.SMEM(cache_len.shape[::-1], jnp.int32),
            dma((5,)),
            dma((4,)),
            dma((STEPS,)),
            dma((STEPS, n)),
            dma((STEPS, n)),
            dma((CHUNKS,)),
            dma((CHUNKS,)),
        ],
        compiler_params=pltpu.CompilerParams(
            collective_id=0, has_side_effects=True, vmem_limit_bytes=62 * 2**20
        ),
    )(incoming, fresh, w_uvqk, w_out, cache_kv, rows_user, cache_len.T)


def solution(mesh):
    in_specs = (
        P("pipe", "ctx", None),
        P("ctx", None),
        P("pipe", None, None),
        P("pipe", None, None),
        P("pipe", None, "ctx", None),
        P(None, "ctx"),
        P(),
    )
    out_specs = P("pipe", None, "ctx", None)
    return jax.shard_map(body, mesh=mesh, in_specs=in_specs, out_specs=out_specs, check_vma=False)
```

```python
import functools

import jax
import jax.numpy as jnp
from jax import lax
from jax.experimental import pallas as pl
from jax.experimental.pallas import tpu as pltpu
from jax.sharding import PartitionSpec as P

HEADS = 4
STEPS = 2
CHUNKS = 4
MESH = pl.DeviceIdType.MESH


def normalize(values):
    center = jnp.mean(values, axis=-1, keepdims=True)
    shifted = values - center
    spread = jnp.mean(shifted * shifted, axis=-1, keepdims=True)
    return shifted * lax.rsqrt(spread + 1e-06)


def silu(values):
    half = 0.5 * values
    return half + half * jnp.tanh(half)


def kernel(
    sections, n, stride,
    incoming, fresh, w_in, w_out, cache, users_in, lengths_in,
    result,
    x_buf, w_buf, wo_buf, kv, q_buf, users_ref, lengths_ref,
    load_sem, w_sem, own_sem, cache_send, cache_recv, relay_send, relay_recv,
):
    section = lax.axis_index("pipe")
    me = lax.axis_index("ctx")
    rows = x_buf.shape[1]
    width = wo_buf.shape[0]
    depth = wo_buf.shape[1]
    piece = depth // CHUNKS
    part = cache.shape[2]
    cached = n * part
    head = width // HEADS
    lines = n // stride
    first = section == 0
    last = section == sections - 1

    x_load = pltpu.make_async_copy(incoming.at[0], x_buf.at[0], load_sem.at[0])
    x_load.start()
    users_load = pltpu.make_async_copy(users_in, users_ref, load_sem.at[3])
    lengths_load = pltpu.make_async_copy(lengths_in, lengths_ref, load_sem.at[4])
    users_load.start()
    lengths_load.start()
    fresh_load = pltpu.make_async_copy(fresh, x_buf.at[1], load_sem.at[1])

    @pl.when(first)
    def _():
        fresh_load.start()

    def w_load(block):
        columns = pl.ds(block * width, width)
        return pltpu.make_async_copy(
            w_in.at[0, :, columns], w_buf.at[:, columns], w_sem.at[block]
        )

    wo_load = pltpu.make_async_copy(w_out.at[0], wo_buf, load_sem.at[2])
    for block in (2, 3, 1, 0):
        w_load(block).start()
    wo_load.start()

    def place(owner):
        return pl.ds(pl.multiple_of(owner * part, part), part)

    own = [
        pltpu.make_async_copy(cache.at[0, t], kv.at[t, place(me), :], own_sem.at[t])
        for t in range(STEPS)
    ]
    for copy in own:
        copy.start()

    lane = lax.rem(me, stride)
    group = me - lane

    def along(hop):
        return lax.rem(me + hop * stride, n)

    def beside(hop):
        return group + lax.rem(lane + hop, stride)

    barrier = pltpu.get_barrier_semaphore()
    for hop in range(1, lines):
        pl.semaphore_signal(barrier, inc=1, device_id={"ctx": along(hop)}, device_id_type=MESH)
    for hop in range(1, stride):
        pl.semaphore_signal(barrier, inc=1, device_id={"ctx": beside(hop)}, device_id_type=MESH)

    @pl.when(jnp.logical_not(last))
    def _():
        pl.semaphore_signal(barrier, inc=1, device_id={"pipe": section + 1}, device_id_type=MESH)

    @pl.when(jnp.logical_not(first))
    def _():
        pl.semaphore_signal(barrier, inc=1, device_id={"pipe": section - 1}, device_id_type=MESH)

    ends = jnp.where(first, 1, 0) + jnp.where(last, 1, 0)
    pl.semaphore_wait(barrier, lines - 1 + stride - 1 + 2 - ends)

    def spread(t, hop):
        slot = hop * stride
        return pltpu.make_async_remote_copy(
            src_ref=cache.at[0, t],
            dst_ref=kv.at[t, place(me), :],
            send_sem=cache_send.at[t, slot],
            recv_sem=cache_recv.at[t, slot],
            device_id={"ctx": along(hop)},
            device_id_type=MESH,
        )

    def spread_arrival(t, hop):
        slot = hop * stride
        owner = lax.rem(me + (lines - hop) * stride, n)
        return pltpu.make_async_remote_copy(
            src_ref=cache.at[0, t],
            dst_ref=kv.at[t, place(owner), :],
            send_sem=cache_send.at[t, slot],
            recv_sem=cache_recv.at[t, slot],
            device_id={"ctx": along(hop)},
            device_id_type=MESH,
        )

    def forward(t, hop, side):
        slot = hop * stride + side
        owner = lax.rem(me + (lines - hop) * stride, n)
        source = cache.at[0, t] if hop == 0 else kv.at[t, place(owner), :]
        return pltpu.make_async_remote_copy(
            src_ref=source,
            dst_ref=kv.at[t, place(owner), :],
            send_sem=cache_send.at[t, slot],
            recv_sem=cache_recv.at[t, slot],
            device_id={"ctx": beside(side)},
            device_id_type=MESH,
        )

    def forward_arrival(t, hop, side):
        slot = hop * stride + side
        owner = lax.rem(beside(stride - side) + (lines - hop) * stride, n)
        return pltpu.make_async_remote_copy(
            src_ref=cache.at[0, t],
            dst_ref=kv.at[t, place(owner), :],
            send_sem=cache_send.at[t, slot],
            recv_sem=cache_recv.at[t, slot],
            device_id={"ctx": beside(side)},
            device_id_type=MESH,
        )

    def send_own(t):
        for hop in range(1, lines):
            spread(t, hop).start()
        for side in range(1, stride):
            forward(t, 0, side).start()

    def pass_on(t):
        for hop in range(1, lines):
            spread_arrival(t, hop).wait_recv()
            for side in range(1, stride):
                forward(t, hop, side).start()

    def arrived(t):
        own[t].wait()
        for hop in range(lines):
            for side in range(1, stride):
                forward_arrival(t, hop, side).wait_recv()

    def relay(c):
        columns = pl.ds(c * piece, piece)
        return pltpu.make_async_remote_copy(
            src_ref=result.at[0, 0, :, columns],
            dst_ref=x_buf.at[1, :, columns],
            send_sem=relay_send.at[c],
            recv_sem=relay_recv.at[c],
            device_id={"pipe": lax.rem(section + 1, sections)},
            device_id_type=MESH,
        )

    def project(normed, block):
        return silu(
            jnp.dot(
                normed,
                w_buf[:, block * width : (block + 1) * width],
                preferred_element_type=jnp.float32,
            )
        ).astype(jnp.bfloat16)

    def allowed_rows(t):
        batch = sections - 1 - section + t
        users = jnp.broadcast_to(users_ref[pl.ds(batch, 1), :], (rows, rows))
        mine = users.T
        row = lax.broadcasted_iota(jnp.int32, (rows, rows), 0)
        column = lax.broadcasted_iota(jnp.int32, (rows, rows), 1)
        new = jnp.where((users == mine) & (column <= row), 1.0, 0.0)
        position = lax.broadcasted_iota(jnp.int32, (rows, cached), 1)
        owner = jnp.zeros((rows, cached), jnp.int32)
        bound = jnp.int32(0)
        for user in range(lengths_ref.shape[0] - 1):
            bound = bound + lengths_ref[user, batch]
            owner = owner + jnp.where(position >= bound, 1, 0)
        old = jnp.where(owner == mine[:, :1], 1.0, 0.0)
        return jnp.concatenate([old, new], axis=1)

    send_own(0)
    send_own(1)
    users_load.wait()
    lengths_load.wait()
    for t in range(STEPS):
        allowed = allowed_rows(t)
        if t == 0:
            x_load.wait()
        else:
            @pl.when(first)
            def _():
                fresh_load.wait()

            @pl.when(jnp.logical_not(first))
            def _():
                for c in range(CHUNKS):
                    relay(c).wait_recv()

        normed = normalize(x_buf[t].astype(jnp.float32)).astype(jnp.bfloat16)
        for block, into in ((2, 0), (3, 1)):
            if t == 0:
                w_load(block).wait()
            kv[t, cached:, into * width : (into + 1) * width] = project(normed, block)
        if t == 0:
            pass_on(0)
            w_load(1).wait()
        q_buf[...] = project(normed, 1)
        if t == 0:
            w_load(0).wait()
        gate = project(normed, 0)
        arrived(t)
        heads = []
        for h in range(HEADS):
            low, high = h * head, (h + 1) * head
            scores = lax.dot_general(
                q_buf[:, low:high],
                kv[t, :, low:high],
                (((1,), (1,)), ((), ())),
                preferred_element_type=jnp.float32,
            )
            weights = (silu(head ** (-0.5) * scores) * allowed).astype(jnp.bfloat16)
            heads.append(
                jnp.dot(
                    weights,
                    kv[t, :, width + low : width + high],
                    preferred_element_type=jnp.float32,
                )
            )
        attn = jnp.concatenate(heads, axis=1)
        mixed = (normalize(attn) * gate.astype(jnp.float32)).astype(jnp.bfloat16)
        if t == 0:
            wo_load.wait()
        for c in range(CHUNKS):
            low, high = c * piece, (c + 1) * piece
            result[0, t, :, low:high] = (
                jnp.dot(mixed, wo_buf[:, low:high], preferred_element_type=jnp.float32)
                + x_buf[t, :, low:high].astype(jnp.float32)
            ).astype(jnp.bfloat16)
            if t == 0:
                @pl.when(jnp.logical_not(last))
                def _():
                    relay(c).start()
        if t == 0:
            pass_on(1)

    for t in range(STEPS):
        for hop in range(lines):
            if hop > 0:
                spread(t, hop).wait_send()
            for side in range(1, stride):
                forward(t, hop, side).wait_send()

    @pl.when(jnp.logical_not(last))
    def _():
        for c in range(CHUNKS):
            relay(c).wait_send()


def body(incoming, fresh, w_uvqk, w_out, cache_kv, rows_user, cache_len):
    sections = lax.axis_size("pipe")
    n = lax.axis_size("ctx")
    stride = 2 if n % 2 == 0 else 1
    rows, depth = fresh.shape
    width = w_out.shape[1]
    part = cache_kv.shape[2]
    anywhere = pl.BlockSpec(memory_space=pltpu.HBM)
    dma = pltpu.SemaphoreType.DMA
    return pl.pallas_call(
        functools.partial(kernel, sections, n, stride),
        out_shape=jax.ShapeDtypeStruct((1, STEPS, rows, depth), jnp.bfloat16),
        in_specs=[anywhere] * 7,
        out_specs=pl.BlockSpec(memory_space=pltpu.VMEM),
        scratch_shapes=[
            pltpu.VMEM((STEPS, rows, depth), jnp.bfloat16),
            pltpu.VMEM((depth, 4 * width), jnp.bfloat16),
            pltpu.VMEM((width, depth), jnp.bfloat16),
            pltpu.VMEM((STEPS, n * part + rows, 2 * width), jnp.bfloat16),
            pltpu.VMEM((rows, width), jnp.bfloat16),
            pltpu.VMEM(rows_user.shape, jnp.int32),
            pltpu.SMEM(cache_len.shape[::-1], jnp.int32),
            dma((5,)),
            dma((4,)),
            dma((STEPS,)),
            dma((STEPS, n)),
            dma((STEPS, n)),
            dma((CHUNKS,)),
            dma((CHUNKS,)),
        ],
        compiler_params=pltpu.CompilerParams(
            collective_id=0, has_side_effects=True, vmem_limit_bytes=40 * 2**20
        ),
    )(
        *(
            pltpu.with_memory_space_constraint(operand, pltpu.HBM)
            for operand in (incoming, fresh, w_uvqk, w_out, cache_kv, rows_user, cache_len.T)
        )
    )


def solution(mesh):
    in_specs = (
        P("pipe", "ctx", None),
        P("ctx", None),
        P("pipe", None, None),
        P("pipe", None, None),
        P("pipe", None, "ctx", None),
        P(None, "ctx"),
        P(),
    )
    out_specs = P("pipe", None, "ctx", None)
    return jax.shard_map(body, mesh=mesh, in_specs=in_specs, out_specs=out_specs, check_vma=False)
```

```python
import functools

import jax
import jax.numpy as jnp
from jax import lax
from jax.experimental import pallas as pl
from jax.experimental.pallas import tpu as pltpu
from jax.sharding import PartitionSpec as P

HEADS = 4
STEPS = 2
CHUNKS = 4
MESH = pl.DeviceIdType.MESH


def normalize(values):
    center = jnp.mean(values, axis=-1, keepdims=True)
    shifted = values - center
    spread = jnp.mean(shifted * shifted, axis=-1, keepdims=True)
    return shifted * lax.rsqrt(spread + 1e-06)


def silu(values):
    half = 0.5 * values
    return half + half * jnp.tanh(half)


def kernel(
    sections, n, stride,
    incoming, fresh, w_in, w_out, cache, users_in, lengths_in,
    result,
    x_buf, w_buf, wo_buf, kv, q_buf, users_ref, lengths_ref,
    load_sem, w_sem, own_sem, cache_send, cache_recv, relay_send, relay_recv,
):
    section = lax.axis_index("pipe")
    me = lax.axis_index("ctx")
    rows = x_buf.shape[1]
    width = wo_buf.shape[0]
    depth = wo_buf.shape[1]
    piece = depth // CHUNKS
    part = cache.shape[2]
    cached = n * part
    head = width // HEADS
    lines = n // stride
    first = section == 0
    last = section == sections - 1

    x_load = pltpu.make_async_copy(incoming.at[0], x_buf.at[0], load_sem.at[0])
    x_load.start()
    users_load = pltpu.make_async_copy(users_in, users_ref, load_sem.at[3])
    lengths_load = pltpu.make_async_copy(lengths_in, lengths_ref, load_sem.at[4])
    users_load.start()
    lengths_load.start()
    fresh_load = pltpu.make_async_copy(fresh, x_buf.at[1], load_sem.at[1])

    @pl.when(first)
    def _():
        fresh_load.start()

    def w_load(block):
        columns = pl.ds(block * width, width)
        return pltpu.make_async_copy(
            w_in.at[0, :, columns], w_buf.at[:, columns], w_sem.at[block]
        )

    wo_load = pltpu.make_async_copy(w_out.at[0], wo_buf, load_sem.at[2])
    w_load(2).start()

    def place(owner):
        return pl.ds(pl.multiple_of(owner * part, part), part)

    own = [
        pltpu.make_async_copy(cache.at[0, t], kv.at[t, place(me), :], own_sem.at[t])
        for t in range(STEPS)
    ]
    for copy in own:
        copy.start()

    lane = lax.rem(me, stride)
    group = me - lane

    def along(hop):
        return lax.rem(me + hop * stride, n)

    def beside(hop):
        return group + lax.rem(lane + hop, stride)

    barrier = pltpu.get_barrier_semaphore()
    for hop in range(1, lines):
        pl.semaphore_signal(barrier, inc=1, device_id={"ctx": along(hop)}, device_id_type=MESH)
    for hop in range(1, stride):
        pl.semaphore_signal(barrier, inc=1, device_id={"ctx": beside(hop)}, device_id_type=MESH)

    @pl.when(jnp.logical_not(last))
    def _():
        pl.semaphore_signal(barrier, inc=1, device_id={"pipe": section + 1}, device_id_type=MESH)

    @pl.when(jnp.logical_not(first))
    def _():
        pl.semaphore_signal(barrier, inc=1, device_id={"pipe": section - 1}, device_id_type=MESH)

    ends = jnp.where(first, 1, 0) + jnp.where(last, 1, 0)
    pl.semaphore_wait(barrier, lines - 1 + stride - 1 + 2 - ends)

    def spread(t, hop):
        slot = hop * stride
        return pltpu.make_async_remote_copy(
            src_ref=cache.at[0, t],
            dst_ref=kv.at[t, place(me), :],
            send_sem=cache_send.at[t, slot],
            recv_sem=cache_recv.at[t, slot],
            device_id={"ctx": along(hop)},
            device_id_type=MESH,
        )

    def spread_arrival(t, hop):
        slot = hop * stride
        owner = lax.rem(me + (lines - hop) * stride, n)
        return pltpu.make_async_remote_copy(
            src_ref=cache.at[0, t],
            dst_ref=kv.at[t, place(owner), :],
            send_sem=cache_send.at[t, slot],
            recv_sem=cache_recv.at[t, slot],
            device_id={"ctx": along(hop)},
            device_id_type=MESH,
        )

    def forward(t, hop, side):
        slot = hop * stride + side
        owner = lax.rem(me + (lines - hop) * stride, n)
        source = cache.at[0, t] if hop == 0 else kv.at[t, place(owner), :]
        return pltpu.make_async_remote_copy(
            src_ref=source,
            dst_ref=kv.at[t, place(owner), :],
            send_sem=cache_send.at[t, slot],
            recv_sem=cache_recv.at[t, slot],
            device_id={"ctx": beside(side)},
            device_id_type=MESH,
        )

    def forward_arrival(t, hop, side):
        slot = hop * stride + side
        owner = lax.rem(beside(stride - side) + (lines - hop) * stride, n)
        return pltpu.make_async_remote_copy(
            src_ref=cache.at[0, t],
            dst_ref=kv.at[t, place(owner), :],
            send_sem=cache_send.at[t, slot],
            recv_sem=cache_recv.at[t, slot],
            device_id={"ctx": beside(side)},
            device_id_type=MESH,
        )

    def send_own(t):
        for hop in range(1, lines):
            spread(t, hop).start()
        for side in range(1, stride):
            forward(t, 0, side).start()

    def pass_on(t):
        for hop in range(1, lines):
            spread_arrival(t, hop).wait_recv()
            for side in range(1, stride):
                forward(t, hop, side).start()

    def arrived(t):
        own[t].wait()
        for hop in range(lines):
            for side in range(1, stride):
                forward_arrival(t, hop, side).wait_recv()

    def relay(c):
        columns = pl.ds(c * piece, piece)
        return pltpu.make_async_remote_copy(
            src_ref=result.at[0, 0, :, columns],
            dst_ref=x_buf.at[1, :, columns],
            send_sem=relay_send.at[c],
            recv_sem=relay_recv.at[c],
            device_id={"pipe": lax.rem(section + 1, sections)},
            device_id_type=MESH,
        )

    def project(normed, block):
        return silu(
            jnp.dot(
                normed,
                w_buf[:, block * width : (block + 1) * width],
                preferred_element_type=jnp.float32,
            )
        ).astype(jnp.bfloat16)

    def allowed_rows(t):
        batch = sections - 1 - section + t
        users = jnp.broadcast_to(users_ref[pl.ds(batch, 1), :], (rows, rows))
        mine = users.T
        row = lax.broadcasted_iota(jnp.int32, (rows, rows), 0)
        column = lax.broadcasted_iota(jnp.int32, (rows, rows), 1)
        new = jnp.where((users == mine) & (column <= row), 1.0, 0.0)
        position = lax.broadcasted_iota(jnp.int32, (rows, cached), 1)
        owner = jnp.zeros((rows, cached), jnp.int32)
        bound = jnp.int32(0)
        for user in range(lengths_ref.shape[0] - 1):
            bound = bound + lengths_ref[user, batch]
            owner = owner + jnp.where(position >= bound, 1, 0)
        old = jnp.where(owner == mine[:, :1], 1.0, 0.0)
        return jnp.concatenate([old, new], axis=1)

    send_own(0)
    for block in (3, 1, 0):
        w_load(block).start()
    wo_load.start()
    send_own(1)
    users_load.wait()
    lengths_load.wait()
    for t in range(STEPS):
        allowed = allowed_rows(t)
        if t == 0:
            x_load.wait()
        else:
            @pl.when(first)
            def _():
                fresh_load.wait()

            @pl.when(jnp.logical_not(first))
            def _():
                for c in range(CHUNKS):
                    relay(c).wait_recv()

        normed = normalize(x_buf[t].astype(jnp.float32)).astype(jnp.bfloat16)
        for block, into in ((2, 0), (3, 1)):
            if t == 0:
                w_load(block).wait()
            kv[t, cached:, into * width : (into + 1) * width] = project(normed, block)
        if t == 0:
            pass_on(0)
            w_load(1).wait()
        q_buf[...] = project(normed, 1)
        if t == 0:
            w_load(0).wait()
        gate = project(normed, 0)
        arrived(t)
        heads = []
        for h in range(HEADS):
            low, high = h * head, (h + 1) * head
            scores = lax.dot_general(
                q_buf[:, low:high],
                kv[t, :, low:high],
                (((1,), (1,)), ((), ())),
                preferred_element_type=jnp.float32,
            )
            weights = (silu(head ** (-0.5) * scores) * allowed).astype(jnp.bfloat16)
            heads.append(
                jnp.dot(
                    weights,
                    kv[t, :, width + low : width + high],
                    preferred_element_type=jnp.float32,
                )
            )
        attn = jnp.concatenate(heads, axis=1)
        mixed = (normalize(attn) * gate.astype(jnp.float32)).astype(jnp.bfloat16)
        if t == 0:
            wo_load.wait()
        for c in range(CHUNKS):
            low, high = c * piece, (c + 1) * piece
            result[0, t, :, low:high] = (
                jnp.dot(mixed, wo_buf[:, low:high], preferred_element_type=jnp.float32)
                + x_buf[t, :, low:high].astype(jnp.float32)
            ).astype(jnp.bfloat16)
            if t == 0:
                @pl.when(jnp.logical_not(last))
                def _():
                    relay(c).start()
        if t == 0:
            pass_on(1)

    for t in range(STEPS):
        for hop in range(lines):
            if hop > 0:
                spread(t, hop).wait_send()
            for side in range(1, stride):
                forward(t, hop, side).wait_send()

    @pl.when(jnp.logical_not(last))
    def _():
        for c in range(CHUNKS):
            relay(c).wait_send()


def body(incoming, fresh, w_uvqk, w_out, cache_kv, rows_user, cache_len):
    sections = lax.axis_size("pipe")
    n = lax.axis_size("ctx")
    stride = 2 if n % 2 == 0 else 1
    rows, depth = fresh.shape
    width = w_out.shape[1]
    part = cache_kv.shape[2]
    anywhere = pl.BlockSpec(memory_space=pltpu.HBM)
    dma = pltpu.SemaphoreType.DMA
    return pl.pallas_call(
        functools.partial(kernel, sections, n, stride),
        out_shape=jax.ShapeDtypeStruct((1, STEPS, rows, depth), jnp.bfloat16),
        in_specs=[anywhere] * 7,
        out_specs=pl.BlockSpec(memory_space=pltpu.VMEM),
        scratch_shapes=[
            pltpu.VMEM((STEPS, rows, depth), jnp.bfloat16),
            pltpu.VMEM((depth, 4 * width), jnp.bfloat16),
            pltpu.VMEM((width, depth), jnp.bfloat16),
            pltpu.VMEM((STEPS, n * part + rows, 2 * width), jnp.bfloat16),
            pltpu.VMEM((rows, width), jnp.bfloat16),
            pltpu.VMEM(rows_user.shape, jnp.int32),
            pltpu.SMEM(cache_len.shape[::-1], jnp.int32),
            dma((5,)),
            dma((4,)),
            dma((STEPS,)),
            dma((STEPS, n)),
            dma((STEPS, n)),
            dma((CHUNKS,)),
            dma((CHUNKS,)),
        ],
        compiler_params=pltpu.CompilerParams(
            collective_id=0, has_side_effects=True, vmem_limit_bytes=40 * 2**20
        ),
    )(
        *(
            pltpu.with_memory_space_constraint(operand, pltpu.HBM)
            for operand in (incoming, fresh, w_uvqk, w_out, cache_kv, rows_user, cache_len.T)
        )
    )


def solution(mesh):
    in_specs = (
        P("pipe", "ctx", None),
        P("ctx", None),
        P("pipe", None, None),
        P("pipe", None, None),
        P("pipe", None, "ctx", None),
        P(None, "ctx"),
        P(),
    )
    out_specs = P("pipe", None, "ctx", None)
    return jax.shard_map(body, mesh=mesh, in_specs=in_specs, out_specs=out_specs, check_vma=False)
```
